32 devices in a mesh: freq: 8 (over y, x, core), node: 4 (over z).
Axes of the slice: x: 2, y: 2, z: 4, core: 2. Of those that a mesh axis runs over, the one named last changes fastest.
Arguments:
- pressure: bfloat16 [2, 128, 4, 8192], P(None, 'freq', None, 'node'), may hold values from -6 to 6
- spectrum_amp: float32 [4, 128], replicated, may hold values from 0.03 to 0.3
- phase_code: int32 [4, 128], replicated, may hold values from 0 to 4095
- panel_tile: int32 [8, 4, 256, 1], P('freq'), may hold values from 0 to 63; in each aligned block of 1024 rows (0 to 1023, 1024 to 2047, ..., all dimensions but the last counted through in order) at most 24 rows name the same one
- patch_weight: bfloat16 [8, 4, 256, 128], P('freq'), may hold values from 0 to 0.099609375
Outputs:
- node_loads: bfloat16 [4, 4096, 8192], P(None, 'node', 'freq')
The draws below stay inside these ranges and needn't reach their ends.
Inputs may be any that keep to these rules, and one draw needn't show every extreme that they name: Within each block panel_tile[g] (1024 panels), no patch is named by more than 24 panels, a bound that some block reaches; every patch is named somewhere.
All inputs are finite; a program needn't handle non-finite values.
Results may differ from the reference program's by a relative error of at most 0.0062.
Values may be sent and summed in bfloat16 or wider, within the bound.
A program may use at most 128 MiB of HBM per device.

```python
import math
import jax
import jax.numpy as jnp
import numpy as np
from jax import lax

F = 128
H = 4
TSTEPS = 4096
BIN_STEP = 15
PHASE_LEVELS = 4096
PAN_DEV = 256
PANELS = 8192
TILES = 64
NODES = 8192
CAPT = 24
N_FREQ = 8
N_NODE = 4


def place_ends(array, rng, least, largest):
    longest = array.shape.index(max(array.shape))
    spots = []
    for shift in (0, 1):
        where = [jax.random.randint(jax.random.fold_in(rng, axis), (), 0, length) for axis, length in enumerate(array.shape)]
        where[longest] = (where[longest] + shift) % array.shape[longest]
        spots.append(tuple(where))
    return array.at[spots[0]].set(least).at[spots[1]].set(largest)


def steps_of(stream_key, extent, split, least, largest):
    level = 1.0
    for axis_at, blocks in split:
        steps = jax.random.uniform(jax.random.fold_in(jax.random.fold_in(stream_key, 6), axis_at), (blocks,), jnp.float32, least / len(split), largest / len(split))
        level = level * jnp.repeat(jnp.exp(steps), extent[axis_at] // blocks).reshape((-1,) + (1,) * (len(extent) - 1 - axis_at))
    return level


def deal_out(rng, own, number, rows, number_of, top, reach, skew):
    ranking = jax.random.permutation(rng, number_of)
    packed, usual = load_shares(number_of, rows * top, reach, skew, True), load_shares(number_of, rows * top, reach, skew, False)
    places = jnp.arange(number_of)

    def named(tallies, rotation):
        used = int((tallies > 0).sum())
        fixed = max(1, used // 4)
        shifted = fixed + (places - fixed + rotation * (used - fixed)) % max(1, number_of - fixed)
        return jnp.zeros((number_of,), jnp.int32).at[ranking[jnp.where(places < fixed, places, shifted)]].set(jnp.asarray(tallies, jnp.int32))

    tallies = jnp.where(number % 4 == 0, named(packed, number // 4), named(usual, number - number // 4 - 1))
    mixed = jax.random.permutation(jax.random.fold_in(own, 3), number_of)
    giver, taker = mixed[0:number_of // 2 * 2:2], mixed[1:number_of // 2 * 2:2]
    room = jnp.minimum(tallies[giver] - 1, reach - tallies[taker]) // 2
    room = jnp.where((giver == ranking[0]) | (taker == ranking[0]) | (tallies[taker] == 0), 0, jnp.maximum(room, 0))
    shifted = jax.random.randint(jax.random.fold_in(own, 4), (number_of // 2,), 0, 1 << 20) % (room + 1)
    tallies = tallies.at[giver].add(-shifted).at[taker].add(shifted)
    labels = jnp.searchsorted(jnp.cumsum(tallies), jnp.arange(rows * top), side="right").astype(jnp.int32)
    grid = labels.reshape(top, rows).T
    grid = grid[jax.random.permutation(jax.random.fold_in(own, 1), rows)]
    rotation = jax.random.randint(jax.random.fold_in(own, 2), (rows, 1), 0, top)
    return jnp.take_along_axis(grid, (jnp.arange(top)[None, :] + rotation) % top, axis=1)


def load_shares(amount, total, reach, skew, full):
    loads = [(1 << 20) // math.isqrt(grade ** skew) + 1 for grade in range(1, amount + 1)]
    largest = reach if full else min(reach, max(-(-total // amount), total * loads[0] // sum(loads)))
    least = 1 if total - largest >= amount - 1 else 0
    given, rest = [largest] + [least] * (amount - 1), total - largest - least * (amount - 1)
    while rest > 0:
        movable = [i for i in range(1, amount) if given[i] < largest] or [i for i in range(1, amount) if given[i] < reach]
        whole, remaining = sum([loads[i] for i in movable]), rest
        for i in movable:
            extra = min(reach - given[i], max(1, remaining * loads[i] // whole), rest)
            given[i] = given[i] + extra
            rest = rest - extra
    return np.array(given)


def centred(key, extent, deviation, limit, pieces=(), held_as=jnp.bfloat16):
    gain = steps_of(key, extent, pieces, -0.22, 0.18) if pieces else 1.0
    array = jax.random.normal(key, extent, jnp.float32) * deviation * gain
    return jnp.minimum(jnp.maximum(array, -limit), limit).astype(held_as)


def setup_inputs(seed: int = 0) -> dict:
    key_list = jax.random.split(jax.random.key(seed), 6)
    pressure = centred(key_list[0], (2, F, H, PANELS), 1.0, 6.0, ((1, 8), (3, 4)))
    spectrum_amp = jnp.clip(jnp.exp(jax.random.uniform(key_list[1], (H, F), jnp.float32, math.log(0.03), math.log(0.3))), 0.03, 0.3)
    phase_code = place_ends(jax.random.randint(key_list[2], (H, F), 0, PHASE_LEVELS), jax.random.fold_in(key_list[2], 1), 0, PHASE_LEVELS - 1).astype(jnp.int32)
    panel_tile_keys = jax.random.split(jax.random.fold_in(key_list[3], 1), N_FREQ * N_NODE * PAN_DEV // (N_NODE * PAN_DEV))
    panel_tile_turns = jax.random.permutation(jax.random.fold_in(key_list[3], 3), N_FREQ * N_NODE * PAN_DEV // (N_NODE * PAN_DEV))
    panel_tile = jax.vmap(lambda own, number: deal_out(jax.random.fold_in(key_list[3], 2), own, number, N_NODE * PAN_DEV, TILES, 1, CAPT, 1))(panel_tile_keys, panel_tile_turns).reshape((N_FREQ, N_NODE, PAN_DEV, 1))
    patch_weight = jnp.clip(0.099609375 * jax.random.uniform(key_list[4], (N_FREQ, N_NODE, PAN_DEV, 128), jnp.float32) ** steps_of(key_list[4], (N_FREQ, N_NODE, PAN_DEV, 128), ((0, 8),), -0.2, 0.2), 0.0, 0.099609375).astype(jnp.bfloat16)
    return {"pressure": pressure, "spectrum_amp": spectrum_amp, "phase_code": phase_code, "panel_tile": panel_tile, "patch_weight": patch_weight}


def scale_spectra(pressure, spectrum_amp, phase_code):
    phase_angle = phase_code.astype(jnp.float32) * (2.0 * math.pi / PHASE_LEVELS)
    amplitude = spectrum_amp.T[:, :, None]
    cosine = jnp.cos(phase_angle).T[:, :, None]
    sine_part = jnp.sin(phase_angle).T[:, :, None]
    real_part = pressure[0].astype(jnp.float32)
    imag_part = pressure[1].astype(jnp.float32)
    scaled_re = amplitude * (real_part * cosine - imag_part * sine_part)
    scaled_im = amplitude * (real_part * sine_part + imag_part * cosine)
    return jnp.stack([scaled_re, scaled_im]).astype(jnp.bfloat16)


def basis_table(first_step, step_count):
    freq_bin = 1 + BIN_STEP * jnp.arange(F, dtype=jnp.int32)
    step_ids = first_step + jnp.arange(step_count, dtype=jnp.int32)
    turn_count = (freq_bin[:, None] * step_ids[None, :]) % TSTEPS
    turn_angle = turn_count.astype(jnp.float32) * (2.0 * math.pi / TSTEPS)
    return jnp.concatenate([jnp.cos(turn_angle), -jnp.sin(turn_angle)], axis=0).astype(jnp.bfloat16)


def reference(pressure, spectrum_amp, phase_code, panel_tile, patch_weight):
    scaled = scale_spectra(pressure, spectrum_amp, phase_code)
    flat_spectra = scaled.reshape(2 * F, H, PANELS).astype(jnp.float32)
    tile_ids = jnp.transpose(panel_tile, (1, 0, 2, 3)).reshape(PANELS).astype(jnp.int32)
    weights = jnp.transpose(patch_weight, (1, 0, 2, 3)).reshape(PANELS, 128)
    per_tile = N_FREQ * CAPT
    onehot = (tile_ids[:, None] == jnp.arange(TILES, dtype=jnp.int32)[None, :]).astype(jnp.int32)
    slot_rank = jnp.sum((jnp.cumsum(onehot, axis=0) - onehot) * onehot, axis=1)
    slot_index = tile_ids * per_tile + slot_rank
    members = jnp.full((TILES * per_tile,), PANELS, jnp.int32).at[slot_index].set(jnp.arange(PANELS, dtype=jnp.int32))
    tile_weight = jnp.take(weights, members, axis=0, mode="fill", fill_value=0)
    tile_weight = tile_weight.reshape(TILES, per_tile, 128).astype(jnp.float32)
    block_len = math.gcd(TSTEPS, 128)

    def one_block(block_index):
        wave_basis = basis_table(block_index * block_len, block_len).astype(jnp.float32)
        series = jnp.einsum('khp,kt->pht', flat_spectra, wave_basis).astype(jnp.bfloat16)
        gathered = jnp.take(series.reshape(PANELS, H * block_len), members, axis=0, mode="fill", fill_value=0)
        gathered = gathered.reshape(TILES, per_tile, H * block_len).astype(jnp.float32)
        partial_value = jnp.einsum('bsr,bsn->rbn', gathered, tile_weight)
        return partial_value.reshape(H, block_len, NODES).astype(jnp.bfloat16)

    block_loads = lax.map(one_block, jnp.arange(TSTEPS // block_len, dtype=jnp.int32))
    return jnp.transpose(block_loads, (1, 0, 2, 3)).reshape(H, TSTEPS, NODES)
```

```python
import functools
import math

import jax
import jax.numpy as jnp
from jax import lax
from jax.experimental import pallas as pl
from jax.experimental.pallas import tpu as pltpu
from jax.sharding import PartitionSpec as P

F = 128
TSTEPS = 4096
BIN_STEP = 15
PHASE_LEVELS = 4096
TILE_DEV = 8
SLOT = 32
MESH = pl.DeviceIdType.MESH


def scale_spectra(pressure, spectrum_amp, phase_code):
    phase_angle = phase_code.astype(jnp.float32) * (2.0 * math.pi / PHASE_LEVELS)
    amplitude = spectrum_amp.T[:, :, None]
    cosine = jnp.cos(phase_angle).T[:, :, None]
    sine_part = jnp.sin(phase_angle).T[:, :, None]
    real_part = pressure[0].astype(jnp.float32)
    imag_part = pressure[1].astype(jnp.float32)
    scaled_re = amplitude * (real_part * cosine - imag_part * sine_part)
    scaled_im = amplitude * (real_part * sine_part + imag_part * cosine)
    return jnp.stack([scaled_re, scaled_im]).astype(jnp.bfloat16)


def basis_table(first_step, step_count):
    freq_bin = 1 + BIN_STEP * jnp.arange(F, dtype=jnp.int32)
    step_ids = first_step + jnp.arange(step_count, dtype=jnp.int32)
    turn_count = freq_bin[:, None] * step_ids[None, :] % TSTEPS
    turn_angle = turn_count.astype(jnp.float32) * (2.0 * math.pi / TSTEPS)
    return jnp.concatenate([jnp.cos(turn_angle), -jnp.sin(turn_angle)], axis=0).astype(jnp.bfloat16)


def basis_rows(first_step, step_count):
    freq_bin = 1 + BIN_STEP * jnp.arange(F, dtype=jnp.int32)
    step_ids = first_step + jnp.arange(step_count, dtype=jnp.int32)
    turn_count = step_ids[:, None] * freq_bin[None, :] % TSTEPS
    turn_angle = turn_count.astype(jnp.float32) * (2.0 * math.pi / TSTEPS)
    return jnp.concatenate([jnp.cos(turn_angle), -jnp.sin(turn_angle)], axis=1).astype(jnp.bfloat16)


def slot_rows(panel_tile):
    tile_ids = panel_tile.reshape(-1)
    count = tile_ids.shape[0]
    order = jnp.arange(count, dtype=jnp.int32)
    same = (tile_ids[:, None] == tile_ids[None, :]) & (order[:, None] < order[None, :])
    rank = jnp.sum(same.astype(jnp.int32), axis=0)
    return (tile_ids * SLOT + rank).reshape(1, count)


def load_kernel(owners, windows, x_ref, w_ref, s_ref, out_ref, xall, wall, sall, pick, xs, ws, block, m,
                z_send, z_recv, w_send, w_recv, s_send, s_recv, m_send, m_recv, own_sem):
    me = lax.axis_index("freq")
    z = lax.axis_index("node")
    rows, panels = x_ref.shape
    part = panels // owners
    groups = xs.shape[0]
    slots = groups * 128
    per_group = 128 // SLOT
    group_dev = groups // owners

    barrier = pltpu.get_barrier_semaphore()
    for d in range(1, owners):
        pl.semaphore_signal(barrier, inc=1, device_id=(lax.rem(me + d, owners), z), device_id_type=MESH)
    for d in range(1, windows):
        pl.semaphore_signal(barrier, inc=1, device_id=(me, lax.rem(z + d, windows)), device_id_type=MESH)
    pl.semaphore_wait(barrier, owners + windows - 2)

    def z_copy(b, source, way, target):
        return pltpu.make_async_remote_copy(
            src_ref=source, dst_ref=xall.at[b], send_sem=z_send.at[way, b], recv_sem=z_recv.at[b],
            device_id=(me, target), device_id_type=MESH)

    def f_copy(source, dest, sends, recvs, d):
        return pltpu.make_async_remote_copy(
            src_ref=source, dst_ref=dest, send_sem=sends.at[d], recv_sem=recvs.at[d],
            device_id=(lax.rem(me + d, owners), z), device_id_type=MESH)

    @pl.when(z + 1 < windows)
    def _():
        z_copy(z, x_ref, 0, z + 1).start()

    @pl.when(z > 0)
    def _():
        z_copy(z, x_ref, 1, z - 1).start()

    for d in range(1, owners):
        f_copy(s_ref, sall.at[me], s_send, s_recv, d).start()
    for d in range(1, owners):
        f_copy(w_ref, wall.at[me], w_send, w_recv, d).start()

    sall[pl.ds(me, 1)] = s_ref[...][None]
    wall[pl.ds(me, 1)] = w_ref[...][None]

    for d in range(1, owners):
        f_copy(s_ref, sall.at[lax.rem(me + owners - d, owners)], s_send, s_recv, d).wait_recv()

    step = 256

    def build(index, carry):
        g = index // (slots // step)
        first = pl.multiple_of(lax.rem(index, slots // step) * step, step)
        ids = first + lax.broadcasted_iota(jnp.int32, (step, sall.shape[2]), 0)
        pick[g, pl.ds(first, step)] = jnp.where(ids == sall[g], 1.0, 0.0).astype(jnp.bfloat16)
        return carry

    lax.fori_loop(0, owners * (slots // step), build, 0)

    def place(source, b, fresh):
        cols = pl.ds(pl.multiple_of(b * part, part), part)

        def one(g, carry):
            x = source[:, pl.ds(pl.multiple_of(g * part, part), part)]
            got = lax.dot_general(x, pick[g, :, cols], (((1,), (1,)), ((), ())),
                                  preferred_element_type=jnp.float32).astype(jnp.bfloat16)
            lanes = pl.ds(pl.multiple_of(g * 128, 128), 128)
            for u in range(groups):
                piece = got[:, u * 128:(u + 1) * 128]
                if fresh:
                    xs[u, :, lanes] = piece
                else:
                    xs[u, :, lanes] = xs[u, :, lanes] + piece
            return carry

        lax.fori_loop(0, owners, one, 0)

    def weigh(g):
        lanes = pl.ds(pl.multiple_of(g * 128, 128), 128)

        def one(index, carry):
            first = pl.multiple_of(index * step, step)
            got = jnp.dot(pick[g, pl.ds(first, step)], wall[g], preferred_element_type=jnp.float32)
            got = got.astype(jnp.bfloat16)
            for half in range(step // 128):
                ws[index * (step // 128) + half, lanes] = got[half * 128:(half + 1) * 128]
            return carry

        lax.fori_loop(0, slots // step, one, 0)

    def arrive(s):
        low, high = z - s, z + s

        @pl.when(low >= 0)
        def _():
            z_copy(low, xall.at[low], 0, z).wait_recv()

            @pl.when(z + 1 < windows)
            def _():
                z_copy(low, xall.at[low], 0, z + 1).start()

        @pl.when(high < windows)
        def _():
            z_copy(high, xall.at[high], 1, z).wait_recv()

            @pl.when(z > 0)
            def _():
                z_copy(high, xall.at[high], 1, z - 1).start()

        @pl.when(low >= 0)
        def _():
            place(xall.at[low], low, False)

        @pl.when(high < windows)
        def _():
            place(xall.at[high], high, False)

    place(x_ref, z, True)
    for s in range(1, windows - 1):
        arrive(s)
    weigh(me)
    for d in range(1, owners):
        src = lax.rem(me + owners - d, owners)
        f_copy(w_ref, wall.at[src], w_send, w_recv, d).wait_recv()
        weigh(src)
    arrive(windows - 1)

    part_of = lax.rem(lax.broadcasted_iota(jnp.int32, (owners * 128, 128), 0) // SLOT, per_group)

    def gather_loads(target):
        def one(e, carry):
            u = target * group_dev + e
            w = ws[u]
            for tt in range(per_group):
                block[:, tt * 128:(tt + 1) * 128] = jnp.where(part_of == tt, w, jnp.zeros_like(w))
            wide = per_group * 128
            got = jnp.dot(xs[u], block[...], preferred_element_type=jnp.float32).astype(jnp.bfloat16)
            m[target, :, :, :, pl.ds(pl.multiple_of(e * wide, wide), wide)] = got.reshape(m.shape[1:4] + (wide,))
            return carry

        lax.fori_loop(0, group_dev, one, 0)

    def m_copy(d):
        target = lax.rem(me + d, owners)
        return pltpu.make_async_remote_copy(
            src_ref=m.at[target], dst_ref=out_ref.at[:, :, me], send_sem=m_send.at[d], recv_sem=m_recv.at[d],
            device_id=(target, z), device_id_type=MESH)

    for d in range(1, owners):
        gather_loads(lax.rem(me + d, owners))
        m_copy(d).start()
    gather_loads(me)
    own = pltpu.make_async_copy(m.at[me], out_ref.at[:, :, me], own_sem)
    own.start()
    own.wait()

    for d in range(1, owners):
        src = lax.rem(me + owners - d, owners)
        pltpu.make_async_remote_copy(
            src_ref=m.at[src], dst_ref=out_ref.at[:, :, src], send_sem=m_send.at[d], recv_sem=m_recv.at[d],
            device_id=(src, z), device_id_type=MESH).wait_recv()
    for d in range(1, owners):
        f_copy(s_ref, sall.at[me], s_send, s_recv, d).wait_send()
        f_copy(w_ref, wall.at[me], w_send, w_recv, d).wait_send()
        m_copy(d).wait_send()
    for s in range(windows):
        low, high = z - s, z + s

        @pl.when((low >= 0) & (z + 1 < windows))
        def _():
            z_copy(low, x_ref, 0, z + 1).wait_send()

        @pl.when((high < windows) & (z > 0))
        def _():
            z_copy(high, x_ref, 1, z - 1).wait_send()


def node_spectra(x, w, s, owners, windows, headings, freqs):
    rows, panels = x.shape
    groups = owners * TILE_DEV * SLOT // 128
    length = w.shape[0]
    dma = pltpu.SemaphoreType.DMA
    vmem = pl.BlockSpec(memory_space=pltpu.VMEM)
    nodes = TILE_DEV * 128
    return pl.pallas_call(
        functools.partial(load_kernel, owners, windows),
        out_shape=jax.ShapeDtypeStruct((headings, 2, owners, freqs, nodes), jnp.bfloat16),
        in_specs=[vmem] * 3,
        out_specs=vmem,
        scratch_shapes=[
            pltpu.VMEM((windows, rows, panels), jnp.bfloat16),
            pltpu.VMEM((owners, length, 128), jnp.bfloat16),
            pltpu.VMEM((owners, 1, length), jnp.int32),
            pltpu.VMEM((owners, groups * 128, length), jnp.bfloat16),
            pltpu.VMEM((groups, rows, owners * 128), jnp.bfloat16),
            pltpu.VMEM((groups, owners * 128, 128), jnp.bfloat16),
            pltpu.VMEM((owners * 128, 128 // SLOT * 128), jnp.bfloat16),
            pltpu.VMEM((owners, headings, 2, freqs, nodes), jnp.bfloat16),
            dma((2, windows)), dma((windows,)),
            dma((owners,)), dma((owners,)), dma((owners,)), dma((owners,)), dma((owners,)), dma((owners,)),
            dma(()),
        ],
        compiler_params=pltpu.CompilerParams(
            collective_id=0, has_side_effects=True, vmem_limit_bytes=60 * 1024 * 1024),
        name="node_spectra",
    )(x, w, s)


def series_kernel(basis_ref, m_ref, out_ref):
    out_ref[0] = jnp.dot(basis_ref[...], m_ref[0], preferred_element_type=jnp.float32).astype(out_ref.dtype)


def load_series(basis, m):
    steps, depth = basis.shape
    headings, _, nodes = m.shape
    tall = 512
    return pl.pallas_call(
        series_kernel,
        grid=(headings, steps // tall),
        out_shape=jax.ShapeDtypeStruct((headings, steps, nodes), jnp.bfloat16),
        in_specs=[pl.BlockSpec((tall, depth), lambda h, t: (t, 0)),
                  pl.BlockSpec((1, depth, nodes), lambda h, t: (h, 0, 0))],
        out_specs=pl.BlockSpec((1, tall, nodes), lambda h, t: (h, t, 0)),
        compiler_params=pltpu.CompilerParams(vmem_limit_bytes=32 * 1024 * 1024),
        name="load_series",
    )(basis, m)


def slot_members(tile_ids, tile_count, capacity):
    row_count = tile_ids.shape[0]
    onehot = (tile_ids[:, None] == jnp.arange(tile_count, dtype=jnp.int32)[None, :]).astype(
        jnp.int32
    )
    slot_rank = jnp.sum((jnp.cumsum(onehot, axis=0) - onehot) * onehot, axis=1)
    slot_index = tile_ids * capacity + slot_rank
    empty = jnp.full((tile_count * capacity,), row_count, jnp.int32)
    return empty.at[slot_index].set(jnp.arange(row_count, dtype=jnp.int32))


def wide_shards(pressure, spectrum_amp, phase_code, panel_tile, patch_weight):
    regrouped = lax.all_to_all(pressure, "freq", split_axis=3, concat_axis=1, tiled=True)
    scaled = scale_spectra(regrouped, spectrum_amp, phase_code)
    freq_count = scaled.shape[1]
    headings = scaled.shape[2]
    panels = scaled.shape[3]
    owners = lax.axis_size("freq")
    windows = lax.axis_size("node")
    window_len = TSTEPS // windows
    first_step = lax.axis_index("node") * window_len
    tile_count = owners * TILE_DEV
    capacity = max(2, 3 * windows * panels // (2 * TILE_DEV * owners))
    tile_ids = panel_tile.reshape(-1)
    weights = patch_weight.reshape(-1, 128)
    members = slot_members(tile_ids, tile_count, capacity)
    sent_weight = jnp.take(weights, members, axis=0, mode="fill", fill_value=0)
    sent_weight = sent_weight.reshape(1, owners, TILE_DEV, capacity, 128)
    spectra = lax.all_gather(scaled, "node", axis=3, tiled=True)
    sent_spectra = jnp.take(spectra, members, axis=3, mode="fill", fill_value=0)
    sent_spectra = sent_spectra.reshape(2 * freq_count * headings, owners, TILE_DEV, capacity)
    wave_basis = basis_table(first_step, window_len)
    got_spectra = lax.all_to_all(sent_spectra, "freq", split_axis=1, concat_axis=1, tiled=True)
    got_weight = lax.all_to_all(sent_weight, "freq", split_axis=1, concat_axis=1, tiled=True)
    shaped = got_spectra.reshape((2 * freq_count, headings) + got_spectra.shape[1:])
    series = jnp.einsum(
        "qhskc,qt->hskct", shaped, wave_basis, preferred_element_type=jnp.float32
    ).astype(jnp.bfloat16)
    partial_value = jnp.einsum(
        "hskct,skcn->htkn", series, got_weight[0], preferred_element_type=jnp.float32
    )
    node_loads = partial_value.reshape(partial_value.shape[0], partial_value.shape[1], -1)
    return node_loads.astype(jnp.bfloat16)


def shards(pressure, spectrum_amp, phase_code, panel_tile, patch_weight):
    owners = lax.axis_size("freq")
    windows = lax.axis_size("node")
    length = panel_tile.shape[1] * panel_tile.shape[2]
    capacity = 3 * length // (2 * TILE_DEV * owners)
    pick_bytes = owners * owners * TILE_DEV * SLOT * length * 2
    if capacity > SLOT or pick_bytes > 34 * 1024 * 1024:
        return wide_shards(pressure, spectrum_amp, phase_code, panel_tile, patch_weight)
    freqs, headings, panels = pressure.shape[1:]
    first = lax.axis_index("freq") * freqs
    amp = lax.dynamic_slice_in_dim(spectrum_amp, first, freqs, 1)
    code = lax.dynamic_slice_in_dim(phase_code, first, freqs, 1)
    scaled = scale_spectra(pressure, amp, code)
    x = jnp.transpose(scaled, (2, 0, 1, 3)).reshape(headings * 2 * freqs, panels)
    m = node_spectra(x, patch_weight.reshape(length, 128), slot_rows(panel_tile), owners, windows, headings, freqs)
    window_len = TSTEPS // windows
    basis = basis_rows(lax.axis_index("node") * window_len, window_len)
    return load_series(basis, m.reshape(headings, 2 * F, TILE_DEV * 128))


def solution(mesh):
    placed = (
        P(None, "freq", None, "node"),
        P(),
        P(),
        P("freq", None, None, None),
        P("freq", None, None, None),
    )
    return jax.shard_map(
        shards, mesh=mesh, in_specs=placed, out_specs=P(None, "node", "freq"), check_vma=False
    )
```

```python
import functools
import math

import jax
import jax.numpy as jnp
from jax import lax
from jax.experimental import pallas as pl
from jax.experimental.pallas import tpu as pltpu
from jax.sharding import PartitionSpec as P

F = 128
TSTEPS = 4096
BIN_STEP = 15
PHASE_LEVELS = 4096
TILE_DEV = 8
SLOT = 32
MESH = pl.DeviceIdType.MESH


def scale_spectra(pressure, spectrum_amp, phase_code):
    phase_angle = phase_code.astype(jnp.float32) * (2.0 * math.pi / PHASE_LEVELS)
    amplitude = spectrum_amp.T[:, :, None]
    cosine = jnp.cos(phase_angle).T[:, :, None]
    sine_part = jnp.sin(phase_angle).T[:, :, None]
    real_part = pressure[0].astype(jnp.float32)
    imag_part = pressure[1].astype(jnp.float32)
    scaled_re = amplitude * (real_part * cosine - imag_part * sine_part)
    scaled_im = amplitude * (real_part * sine_part + imag_part * cosine)
    return jnp.stack([scaled_re, scaled_im]).astype(jnp.bfloat16)


def basis_table(first_step, step_count):
    freq_bin = 1 + BIN_STEP * jnp.arange(F, dtype=jnp.int32)
    step_ids = first_step + jnp.arange(step_count, dtype=jnp.int32)
    turn_count = freq_bin[:, None] * step_ids[None, :] % TSTEPS
    turn_angle = turn_count.astype(jnp.float32) * (2.0 * math.pi / TSTEPS)
    return jnp.concatenate([jnp.cos(turn_angle), -jnp.sin(turn_angle)], axis=0).astype(jnp.bfloat16)


def basis_rows(first_step, step_count):
    freq_bin = 1 + BIN_STEP * jnp.arange(F, dtype=jnp.int32)
    step_ids = first_step + jnp.arange(step_count, dtype=jnp.int32)
    turn_count = step_ids[:, None] * freq_bin[None, :] % TSTEPS
    turn_angle = turn_count.astype(jnp.float32) * (2.0 * math.pi / TSTEPS)
    return jnp.concatenate([jnp.cos(turn_angle), -jnp.sin(turn_angle)], axis=1).astype(jnp.bfloat16)


def slot_rows(panel_tile):
    tile_ids = panel_tile.reshape(-1)
    count = tile_ids.shape[0]
    order = jnp.arange(count, dtype=jnp.int32)
    same = (tile_ids[:, None] == tile_ids[None, :]) & (order[:, None] < order[None, :])
    rank = jnp.sum(same.astype(jnp.int32), axis=0)
    return (tile_ids * SLOT + rank).reshape(1, count)


def load_kernel(owners, windows, x_ref, w_ref, s_ref, out_ref, xall, sall, cols, xs, ws, block, m,
                z_send, z_recv, w_send, w_recv, o_send, o_recv, s_send, s_recv, m_send, m_recv, own_sem):
    me = lax.axis_index("freq")
    z = lax.axis_index("node")
    rows, panels = x_ref.shape
    part = panels // owners
    groups = xs.shape[0]
    per_group = 128 // SLOT
    group_dev = groups // owners
    chips = owners // 2
    other = me + 1 - 2 * lax.rem(me, 2)

    barrier = pltpu.get_barrier_semaphore()
    for d in range(1, owners):
        pl.semaphore_signal(barrier, inc=1, device_id=(lax.rem(me + d, owners), z), device_id_type=MESH)
    for d in range(1, windows):
        pl.semaphore_signal(barrier, inc=1, device_id=(me, lax.rem(z + d, windows)), device_id_type=MESH)
    pl.semaphore_wait(barrier, owners + windows - 2)

    def z_copy(b, source, way, target):
        return pltpu.make_async_remote_copy(
            src_ref=source, dst_ref=xall.at[b], send_sem=z_send.at[way, b], recv_sem=z_recv.at[b],
            device_id=(me, target), device_id_type=MESH)

    def s_copy(g, d):
        return pltpu.make_async_remote_copy(
            src_ref=s_ref, dst_ref=sall.at[g], send_sem=s_send.at[d], recv_sem=s_recv.at[d],
            device_id=(lax.rem(me + d, owners), z), device_id_type=MESH)

    def lanes_of(g):
        return pl.ds(pl.multiple_of(g * 128, 128), 128)

    def w_copy(g, d):
        held = ws.at[:, lanes_of(g)]
        return pltpu.make_async_remote_copy(
            src_ref=held, dst_ref=held, send_sem=w_send.at[d], recv_sem=w_recv.at[d],
            device_id=(lax.rem(me + 2 * d, owners), z), device_id_type=MESH)

    def o_copy(g, d):
        held = ws.at[:, lanes_of(g)]
        return pltpu.make_async_remote_copy(
            src_ref=held, dst_ref=held, send_sem=o_send.at[d], recv_sem=o_recv.at[d],
            device_id=(other, z), device_id_type=MESH)

    @pl.when(z + 1 < windows)
    def _():
        z_copy(z, x_ref, 0, z + 1).start()

    @pl.when(z > 0)
    def _():
        z_copy(z, x_ref, 1, z - 1).start()

    for d in range(1, owners):
        s_copy(me, d).start()
    sall[pl.ds(me, 1)] = s_ref[...][None]

    def weigh(u, carry):
        ids = u * 128 + lax.broadcasted_iota(jnp.int32, (128, s_ref.shape[1]), 0)
        pick = jnp.where(ids == s_ref[...], 1.0, 0.0).astype(jnp.bfloat16)
        ws[u, lanes_of(me)] = jnp.dot(pick, w_ref[...], preferred_element_type=jnp.float32).astype(jnp.bfloat16)
        return carry

    lax.fori_loop(0, groups, weigh, 0)
    for d in range(1, chips):
        w_copy(me, d).start()
    o_copy(me, 0).start()

    for d in range(1, owners):
        s_copy(lax.rem(me + owners - d, owners), d).wait_recv()

    def column(g, carry):
        row = sall[g].astype(jnp.float32)
        for k in range(row.shape[1] // 128):
            piece = jnp.broadcast_to(row[:, k * 128:(k + 1) * 128], (128, 128))
            cols[g, k * 128:(k + 1) * 128] = piece.T
        return carry

    lax.fori_loop(0, owners, column, 0)

    wide = 256 // 128

    def place(source, b, fresh):
        def one(g, carry):
            x = source[:, pl.ds(pl.multiple_of(g * part, part), part)]
            col = cols[g, pl.ds(pl.multiple_of(b * part, part), part)]
            lane = lax.broadcasted_iota(jnp.int32, col.shape, 1).astype(jnp.float32)
            lanes = lanes_of(g)
            for u in range(0, groups, wide):
                pick = jnp.concatenate(
                    [jnp.where(col == lane + float((u + v) * 128), 1.0, 0.0).astype(jnp.bfloat16) for v in range(wide)],
                    axis=1)
                got = jnp.dot(x, pick, preferred_element_type=jnp.float32).astype(jnp.bfloat16)
                for v in range(wide):
                    piece = got[:, v * 128:(v + 1) * 128]
                    if fresh:
                        xs[u + v, :, lanes] = piece
                    else:
                        xs[u + v, :, lanes] = xs[u + v, :, lanes] + piece
            return carry

        lax.fori_loop(0, owners, one, 0)

    def arrive(s):
        low, high = z - s, z + s

        @pl.when(low >= 0)
        def _():
            z_copy(low, xall.at[low], 0, z).wait_recv()

            @pl.when(z + 1 < windows)
            def _():
                z_copy(low, xall.at[low], 0, z + 1).start()

        @pl.when(high < windows)
        def _():
            z_copy(high, xall.at[high], 1, z).wait_recv()

            @pl.when(z > 0)
            def _():
                z_copy(high, xall.at[high], 1, z - 1).start()

    def settle(s):
        low, high = z - s, z + s

        @pl.when(low >= 0)
        def _():
            place(xall.at[low], low, False)

        @pl.when(high < windows)
        def _():
            place(xall.at[high], high, False)

    def spread():
        part_of = lax.rem(lax.broadcasted_iota(jnp.int32, (128, 128), 0) // SLOT, per_group)

        def one(u, carry):
            for g in range(owners):
                w = ws[u, g * 128:(g + 1) * 128]
                for tt in range(per_group):
                    block[u, g * 128:(g + 1) * 128, tt * 128:(tt + 1) * 128] = jnp.where(
                        part_of == tt, w, jnp.zeros_like(w))
            return carry

        lax.fori_loop(0, groups, one, 0)

    place(x_ref, z, True)
    arrive(1)
    for d in range(1, chips):
        src = lax.rem(me + owners - 2 * d, owners)
        w_copy(src, d).wait_recv()
        o_copy(src, d).start()
    settle(1)
    for s in range(2, windows - 1):
        arrive(s)
        settle(s)
    for d in range(chips):
        o_copy(lax.rem(other + owners - 2 * d, owners), d).wait_recv()
    spread()
    for s in range(max(2, windows - 1), windows):
        arrive(s)
        settle(s)

    def gather_loads(target):
        def one(e, carry):
            u = target * group_dev + e
            width = per_group * 128
            got = jnp.dot(xs[u], block[u], preferred_element_type=jnp.float32).astype(jnp.bfloat16)
            m[target, :, :, :, pl.ds(pl.multiple_of(e * width, width), width)] = got.reshape(m.shape[1:4] + (width,))
            return carry

        lax.fori_loop(0, group_dev, one, 0)

    def m_copy(d):
        target = lax.rem(me + d, owners)
        return pltpu.make_async_remote_copy(
            src_ref=m.at[target], dst_ref=out_ref.at[:, :, me], send_sem=m_send.at[d], recv_sem=m_recv.at[d],
            device_id=(target, z), device_id_type=MESH)

    for d in range(1, owners):
        gather_loads(lax.rem(me + d, owners))
        m_copy(d).start()
    gather_loads(me)
    own = pltpu.make_async_copy(m.at[me], out_ref.at[:, :, me], own_sem)
    own.start()
    own.wait()

    for d in range(1, owners):
        src = lax.rem(me + owners - d, owners)
        pltpu.make_async_remote_copy(
            src_ref=m.at[src], dst_ref=out_ref.at[:, :, src], send_sem=m_send.at[d], recv_sem=m_recv.at[d],
            device_id=(src, z), device_id_type=MESH).wait_recv()
    for d in range(1, owners):
        s_copy(me, d).wait_send()
        m_copy(d).wait_send()
    for d in range(1, chips):
        w_copy(me, d).wait_send()
    for d in range(chips):
        o_copy(me, d).wait_send()
    for s in range(windows):
        low, high = z - s, z + s

        @pl.when((low >= 0) & (z + 1 < windows))
        def _():
            z_copy(low, x_ref, 0, z + 1).wait_send()

        @pl.when((high < windows) & (z > 0))
        def _():
            z_copy(high, x_ref, 1, z - 1).wait_send()


def node_spectra(x, w, s, owners, windows, headings, freqs):
    rows, panels = x.shape
    groups = owners * TILE_DEV * SLOT // 128
    length = w.shape[0]
    dma = pltpu.SemaphoreType.DMA
    vmem = pl.BlockSpec(memory_space=pltpu.VMEM)
    nodes = TILE_DEV * 128
    return pl.pallas_call(
        functools.partial(load_kernel, owners, windows),
        out_shape=jax.ShapeDtypeStruct((headings, 2, owners, freqs, nodes), jnp.bfloat16),
        in_specs=[vmem] * 3,
        out_specs=vmem,
        scratch_shapes=[
            pltpu.VMEM((windows, rows, panels), jnp.bfloat16),
            pltpu.VMEM((owners, 1, length), jnp.int32),
            pltpu.VMEM((owners, length, 128), jnp.float32),
            pltpu.VMEM((groups, rows, owners * 128), jnp.bfloat16),
            pltpu.VMEM((groups, owners * 128, 128), jnp.bfloat16),
            pltpu.VMEM((groups, owners * 128, 128 // SLOT * 128), jnp.bfloat16),
            pltpu.VMEM((owners, headings, 2, freqs, nodes), jnp.bfloat16),
            dma((2, windows)), dma((windows,)),
            dma((owners,)), dma((owners,)), dma((owners,)), dma((owners,)), dma((owners,)), dma((owners,)),
            dma((owners,)), dma((owners,)),
            dma(()),
        ],
        compiler_params=pltpu.CompilerParams(
            collective_id=0, has_side_effects=True, vmem_limit_bytes=56 * 1024 * 1024),
        name="node_spectra",
    )(x, w, s)


def series_kernel(basis_ref, m_ref, out_ref):
    out_ref[0] = jnp.dot(basis_ref[...], m_ref[0], preferred_element_type=jnp.float32).astype(out_ref.dtype)


def load_series(basis, m):
    steps, depth = basis.shape
    headings, _, nodes = m.shape
    tall = 512
    return pl.pallas_call(
        series_kernel,
        grid=(headings, steps // tall),
        out_shape=jax.ShapeDtypeStruct((headings, steps, nodes), jnp.bfloat16),
        in_specs=[pl.BlockSpec((tall, depth), lambda h, t: (t, 0)),
                  pl.BlockSpec((1, depth, nodes), lambda h, t: (h, 0, 0))],
        out_specs=pl.BlockSpec((1, tall, nodes), lambda h, t: (h, t, 0)),
        compiler_params=pltpu.CompilerParams(vmem_limit_bytes=32 * 1024 * 1024),
        name="load_series",
    )(basis, m)


def slot_members(tile_ids, tile_count, capacity):
    row_count = tile_ids.shape[0]
    onehot = (tile_ids[:, None] == jnp.arange(tile_count, dtype=jnp.int32)[None, :]).astype(
        jnp.int32
    )
    slot_rank = jnp.sum((jnp.cumsum(onehot, axis=0) - onehot) * onehot, axis=1)
    slot_index = tile_ids * capacity + slot_rank
    empty = jnp.full((tile_count * capacity,), row_count, jnp.int32)
    return empty.at[slot_index].set(jnp.arange(row_count, dtype=jnp.int32))


def wide_shards(pressure, spectrum_amp, phase_code, panel_tile, patch_weight):
    regrouped = lax.all_to_all(pressure, "freq", split_axis=3, concat_axis=1, tiled=True)
    scaled = scale_spectra(regrouped, spectrum_amp, phase_code)
    freq_count = scaled.shape[1]
    headings = scaled.shape[2]
    panels = scaled.shape[3]
    owners = lax.axis_size("freq")
    windows = lax.axis_size("node")
    window_len = TSTEPS // windows
    first_step = lax.axis_index("node") * window_len
    tile_count = owners * TILE_DEV
    capacity = max(2, 3 * windows * panels // (2 * TILE_DEV * owners))
    tile_ids = panel_tile.reshape(-1)
    weights = patch_weight.reshape(-1, 128)
    members = slot_members(tile_ids, tile_count, capacity)
    sent_weight = jnp.take(weights, members, axis=0, mode="fill", fill_value=0)
    sent_weight = sent_weight.reshape(1, owners, TILE_DEV, capacity, 128)
    spectra = lax.all_gather(scaled, "node", axis=3, tiled=True)
    sent_spectra = jnp.take(spectra, members, axis=3, mode="fill", fill_value=0)
    sent_spectra = sent_spectra.reshape(2 * freq_count * headings, owners, TILE_DEV, capacity)
    wave_basis = basis_table(first_step, window_len)
    got_spectra = lax.all_to_all(sent_spectra, "freq", split_axis=1, concat_axis=1, tiled=True)
    got_weight = lax.all_to_all(sent_weight, "freq", split_axis=1, concat_axis=1, tiled=True)
    shaped = got_spectra.reshape((2 * freq_count, headings) + got_spectra.shape[1:])
    series = jnp.einsum(
        "qhskc,qt->hskct", shaped, wave_basis, preferred_element_type=jnp.float32
    ).astype(jnp.bfloat16)
    partial_value = jnp.einsum(
        "hskct,skcn->htkn", series, got_weight[0], preferred_element_type=jnp.float32
    )
    node_loads = partial_value.reshape(partial_value.shape[0], partial_value.shape[1], -1)
    return node_loads.astype(jnp.bfloat16)


def shards(pressure, spectrum_amp, phase_code, panel_tile, patch_weight):
    owners = lax.axis_size("freq")
    windows = lax.axis_size("node")
    length = panel_tile.shape[1] * panel_tile.shape[2]
    capacity = 3 * length // (2 * TILE_DEV * owners)
    block_bytes = owners * owners * TILE_DEV * SLOT * 128 * (128 // SLOT) * 2
    if capacity > SLOT or block_bytes > 20 * 1024 * 1024:
        return wide_shards(pressure, spectrum_amp, phase_code, panel_tile, patch_weight)
    freqs, headings, panels = pressure.shape[1:]
    first = lax.axis_index("freq") * freqs
    amp = lax.dynamic_slice_in_dim(spectrum_amp, first, freqs, 1)
    code = lax.dynamic_slice_in_dim(phase_code, first, freqs, 1)
    scaled = scale_spectra(pressure, amp, code)
    x = jnp.transpose(scaled, (2, 0, 1, 3)).reshape(headings * 2 * freqs, panels)
    m = node_spectra(x, patch_weight.reshape(length, 128), slot_rows(panel_tile), owners, windows, headings, freqs)
    window_len = TSTEPS // windows
    basis = basis_rows(lax.axis_index("node") * window_len, window_len)
    return load_series(basis, m.reshape(headings, 2 * F, TILE_DEV * 128))


def solution(mesh):
    placed = (
        P(None, "freq", None, "node"),
        P(),
        P(),
        P("freq", None, None, None),
        P("freq", None, None, None),
    )
    return jax.shard_map(
        shards, mesh=mesh, in_specs=placed, out_specs=P(None, "node", "freq"), check_vma=False
    )
```

```python
import functools
import math

import jax
import jax.numpy as jnp
from jax import lax
from jax.experimental import pallas as pl
from jax.experimental.pallas import tpu as pltpu
from jax.sharding import PartitionSpec as P

F = 128
TSTEPS = 4096
BIN_STEP = 15
PHASE_LEVELS = 4096
TILE_DEV = 8
SLOT = 32
MESH = pl.DeviceIdType.MESH


def scale_spectra(pressure, spectrum_amp, phase_code):
    phase_angle = phase_code.astype(jnp.float32) * (2.0 * math.pi / PHASE_LEVELS)
    amplitude = spectrum_amp.T[:, :, None]
    cosine = jnp.cos(phase_angle).T[:, :, None]
    sine_part = jnp.sin(phase_angle).T[:, :, None]
    real_part = pressure[0].astype(jnp.float32)
    imag_part = pressure[1].astype(jnp.float32)
    scaled_re = amplitude * (real_part * cosine - imag_part * sine_part)
    scaled_im = amplitude * (real_part * sine_part + imag_part * cosine)
    return jnp.stack([scaled_re, scaled_im]).astype(jnp.bfloat16)


def basis_table(first_step, step_count):
    freq_bin = 1 + BIN_STEP * jnp.arange(F, dtype=jnp.int32)
    step_ids = first_step + jnp.arange(step_count, dtype=jnp.int32)
    turn_count = freq_bin[:, None] * step_ids[None, :] % TSTEPS
    turn_angle = turn_count.astype(jnp.float32) * (2.0 * math.pi / TSTEPS)
    return jnp.concatenate([jnp.cos(turn_angle), -jnp.sin(turn_angle)], axis=0).astype(jnp.bfloat16)


def basis_rows(first_step, step_count):
    freq_bin = 1 + BIN_STEP * jnp.arange(F, dtype=jnp.int32)
    step_ids = first_step + jnp.arange(step_count, dtype=jnp.int32)
    turn_count = step_ids[:, None] * freq_bin[None, :] % TSTEPS
    turn_angle = turn_count.astype(jnp.float32) * (2.0 * math.pi / TSTEPS)
    return jnp.concatenate([jnp.cos(turn_angle), -jnp.sin(turn_angle)], axis=1).astype(jnp.bfloat16)


def slot_rows(panel_tile):
    tile_ids = panel_tile.reshape(-1)
    count = tile_ids.shape[0]
    order = jnp.arange(count, dtype=jnp.int32)
    same = (tile_ids[:, None] == tile_ids[None, :]) & (order[:, None] < order[None, :])
    rank = jnp.sum(same.astype(jnp.int32), axis=0)
    return (tile_ids * SLOT + rank).reshape(1, count)


def load_kernel(owners, windows, x_ref, w_ref, s_ref, out_ref, xall, sall, cols, xs, ws, block, m,
                z_send, z_recv, w_send, w_recv, o_send, o_recv, s_send, s_recv, m_send, m_recv, own_sem):
    me = lax.axis_index("freq")
    z = lax.axis_index("node")
    rows, panels = x_ref.shape
    part = panels // owners
    groups = xs.shape[0]
    per_group = 128 // SLOT
    group_dev = groups // owners
    chips = owners // 2
    other = me + 1 - 2 * lax.rem(me, 2)

    barrier = pltpu.get_barrier_semaphore()
    for d in range(1, owners):
        pl.semaphore_signal(barrier, inc=1, device_id=(lax.rem(me + d, owners), z), device_id_type=MESH)
    for d in range(1, windows):
        pl.semaphore_signal(barrier, inc=1, device_id=(me, lax.rem(z + d, windows)), device_id_type=MESH)
    pl.semaphore_wait(barrier, owners + windows - 2)

    headings = m.shape[1]
    each = rows // headings
    cuts = [0, headings // 2, headings] if headings > 1 else [0, headings]
    chunks = len(cuts) - 1

    def rows_of(c):
        return slice(cuts[c] * each, cuts[c + 1] * each)

    def z_copy(c, b, source, way, target):
        return pltpu.make_async_remote_copy(
            src_ref=source.at[rows_of(c)], dst_ref=xall.at[b, rows_of(c)], send_sem=z_send.at[way, c, b],
            recv_sem=z_recv.at[c, b], device_id=(me, target), device_id_type=MESH)

    def own_up(c):
        z_copy(c, z, x_ref, 0, z + 1).start()

    def own_down(c):
        z_copy(c, z, x_ref, 1, z - 1).start()

    def s_copy(g, d):
        return pltpu.make_async_remote_copy(
            src_ref=s_ref, dst_ref=sall.at[g], send_sem=s_send.at[d], recv_sem=s_recv.at[d],
            device_id=(lax.rem(me + d, owners), z), device_id_type=MESH)

    def lanes_of(g):
        return pl.ds(pl.multiple_of(g * 128, 128), 128)

    def w_copy(g, d):
        held = ws.at[:, lanes_of(g)]
        return pltpu.make_async_remote_copy(
            src_ref=held, dst_ref=held, send_sem=w_send.at[d], recv_sem=w_recv.at[d],
            device_id=(lax.rem(me + 2 * d, owners), z), device_id_type=MESH)

    def o_copy(g, d):
        held = ws.at[:, lanes_of(g)]
        return pltpu.make_async_remote_copy(
            src_ref=held, dst_ref=held, send_sem=o_send.at[d], recv_sem=o_recv.at[d],
            device_id=(other, z), device_id_type=MESH)

    @pl.when(z + 1 < windows)
    def _():
        own_up(0)

    @pl.when(z > 0)
    def _():
        own_down(0)

    for d in range(1, owners):
        s_copy(me, d).start()
    sall[pl.ds(me, 1)] = s_ref[...][None]

    def weigh(u, carry):
        ids = u * 128 + lax.broadcasted_iota(jnp.int32, (128, s_ref.shape[1]), 0)
        pick = jnp.where(ids == s_ref[...], 1.0, 0.0).astype(jnp.bfloat16)
        ws[u, lanes_of(me)] = jnp.dot(pick, w_ref[...], preferred_element_type=jnp.float32).astype(jnp.bfloat16)
        return carry

    lax.fori_loop(0, groups, weigh, 0)
    for d in range(1, chips):
        w_copy(me, d).start()
    o_copy(me, 0).start()

    for d in range(1, owners):
        s_copy(lax.rem(me + owners - d, owners), d).wait_recv()

    def column(g, carry):
        row = sall[g].astype(jnp.float32)
        for k in range(row.shape[1] // 128):
            piece = jnp.broadcast_to(row[:, k * 128:(k + 1) * 128], (128, 128))
            cols[g, k * 128:(k + 1) * 128] = piece.T
        return carry

    lax.fori_loop(0, owners, column, 0)

    wide = 256 // 128

    def place(c, source, b, fresh):
        held = rows_of(c)

        def one(g, carry):
            x = source[held, pl.ds(pl.multiple_of(g * part, part), part)]
            col = cols[g, pl.ds(pl.multiple_of(b * part, part), part)]
            lane = lax.broadcasted_iota(jnp.int32, col.shape, 1).astype(jnp.float32)
            lanes = lanes_of(g)
            for u in range(0, groups, wide):
                pick = jnp.concatenate(
                    [jnp.where(col == lane + float((u + v) * 128), 1.0, 0.0).astype(jnp.bfloat16) for v in range(wide)],
                    axis=1)
                got = jnp.dot(x, pick, preferred_element_type=jnp.float32).astype(jnp.bfloat16)
                for v in range(wide):
                    piece = got[:, v * 128:(v + 1) * 128]
                    if fresh:
                        xs[u + v, held, lanes] = piece
                    else:
                        xs[u + v, held, lanes] = xs[u + v, held, lanes] + piece
            return carry

        lax.fori_loop(0, owners, one, 0)

    def arrive(c, s):
        low, high = z - s, z + s

        @pl.when(low >= 0)
        def _():
            z_copy(c, low, xall.at[low], 0, z).wait_recv()

            @pl.when(z + 1 < windows)
            def _():
                z_copy(c, low, xall.at[low], 0, z + 1).start()

        @pl.when(high < windows)
        def _():
            z_copy(c, high, xall.at[high], 1, z).wait_recv()

            @pl.when(z > 0)
            def _():
                z_copy(c, high, xall.at[high], 1, z - 1).start()

        if c + 1 < chunks:
            up_now = z == s
            down_now = windows - 1 - z == s
            if s == 1:
                up_now = up_now | (z == 0)
                down_now = down_now | (z == windows - 1)

            @pl.when(up_now & (z + 1 < windows))
            def _():
                own_up(c + 1)

            @pl.when(down_now & (z > 0))
            def _():
                own_down(c + 1)

    def settle(c, s):
        low, high = z - s, z + s

        @pl.when(low >= 0)
        def _():
            place(c, xall.at[low], low, False)

        @pl.when(high < windows)
        def _():
            place(c, xall.at[high], high, False)

    def spread():
        part_of = lax.rem(lax.broadcasted_iota(jnp.int32, (128, 128), 0) // SLOT, per_group)

        def one(u, carry):
            for g in range(owners):
                w = ws[u, g * 128:(g + 1) * 128]
                for tt in range(per_group):
                    block[u, g * 128:(g + 1) * 128, tt * 128:(tt + 1) * 128] = jnp.where(
                        part_of == tt, w, jnp.zeros_like(w))
            return carry

        lax.fori_loop(0, groups, one, 0)

    def gather_loads(c, target):
        def one(e, carry):
            u = target * group_dev + e
            width = per_group * 128
            got = jnp.dot(xs[u, rows_of(c)], block[u], preferred_element_type=jnp.float32).astype(jnp.bfloat16)
            m[target, cuts[c]:cuts[c + 1], :, :, pl.ds(pl.multiple_of(e * width, width), width)] = got.reshape(
                (cuts[c + 1] - cuts[c],) + m.shape[2:4] + (width,))
            return carry

        lax.fori_loop(0, group_dev, one, 0)

    def m_copy(c, d, source, dest, device):
        return pltpu.make_async_remote_copy(
            src_ref=m.at[source, cuts[c]:cuts[c + 1]], dst_ref=out_ref.at[cuts[c]:cuts[c + 1], :, dest],
            send_sem=m_send.at[c, d], recv_sem=m_recv.at[c, d], device_id=(device, z), device_id_type=MESH)

    def sent(c, d):
        target = lax.rem(me + d, owners)
        return m_copy(c, d, target, me, target)

    def hand_out(c):
        for d in range(1, owners):
            gather_loads(c, lax.rem(me + d, owners))
            sent(c, d).start()
        gather_loads(c, me)

    for c in range(chunks):
        place(c, x_ref, z, True)
        for s in range(1, windows):
            arrive(c, s)
            if c == 1 and s == 1:
                for d in range(chips):
                    o_copy(lax.rem(other + owners - 2 * d, owners), d).wait_recv()
                spread()
                hand_out(0)
            settle(c, s)
        if c == 0:
            for d in range(1, chips):
                src = lax.rem(me + owners - 2 * d, owners)
                w_copy(src, d).wait_recv()
                o_copy(src, d).start()
        if chunks == 1:
            for d in range(chips):
                o_copy(lax.rem(other + owners - 2 * d, owners), d).wait_recv()
            spread()
        if c or chunks == 1:
            hand_out(c)
    own = pltpu.make_async_copy(m.at[me], out_ref.at[:, :, me], own_sem)
    own.start()
    own.wait()

    for c in range(chunks):
        for d in range(1, owners):
            src = lax.rem(me + owners - d, owners)
            m_copy(c, d, src, src, src).wait_recv()
            sent(c, d).wait_send()
    for d in range(1, owners):
        s_copy(me, d).wait_send()
    for d in range(1, chips):
        w_copy(me, d).wait_send()
    for d in range(chips):
        o_copy(me, d).wait_send()
    for s in range(windows):
        low, high = z - s, z + s

        @pl.when((low >= 0) & (z + 1 < windows))
        def _():
            for c in range(chunks):
                z_copy(c, low, x_ref, 0, z + 1).wait_send()

        @pl.when((high < windows) & (z > 0))
        def _():
            for c in range(chunks):
                z_copy(c, high, x_ref, 1, z - 1).wait_send()


def node_spectra(x, w, s, owners, windows, headings, freqs):
    rows, panels = x.shape
    groups = owners * TILE_DEV * SLOT // 128
    length = w.shape[0]
    dma = pltpu.SemaphoreType.DMA
    vmem = pl.BlockSpec(memory_space=pltpu.VMEM)
    nodes = TILE_DEV * 128
    return pl.pallas_call(
        functools.partial(load_kernel, owners, windows),
        out_shape=jax.ShapeDtypeStruct((headings, 2, owners, freqs, nodes), jnp.bfloat16),
        in_specs=[vmem] * 3,
        out_specs=vmem,
        scratch_shapes=[
            pltpu.VMEM((windows, rows, panels), jnp.bfloat16),
            pltpu.VMEM((owners, 1, length), jnp.int32),
            pltpu.VMEM((owners, length, 128), jnp.float32),
            pltpu.VMEM((groups, rows, owners * 128), jnp.bfloat16),
            pltpu.VMEM((groups, owners * 128, 128), jnp.bfloat16),
            pltpu.VMEM((groups, owners * 128, 128 // SLOT * 128), jnp.bfloat16),
            pltpu.VMEM((owners, headings, 2, freqs, nodes), jnp.bfloat16),
            dma((2, headings, windows)), dma((headings, windows)),
            dma((owners,)), dma((owners,)), dma((owners,)), dma((owners,)), dma((owners,)), dma((owners,)),
            dma((headings, owners)), dma((headings, owners)),
            dma(()),
        ],
        compiler_params=pltpu.CompilerParams(
            collective_id=0, has_side_effects=True, vmem_limit_bytes=56 * 1024 * 1024),
        name="node_spectra",
    )(x, w, s)


def series_kernel(basis_ref, m_ref, out_ref):
    out_ref[0] = jnp.dot(basis_ref[...], m_ref[0], preferred_element_type=jnp.float32).astype(out_ref.dtype)


def load_series(basis, m):
    steps, depth = basis.shape
    headings, _, nodes = m.shape
    tall = 512
    return pl.pallas_call(
        series_kernel,
        grid=(headings, steps // tall),
        out_shape=jax.ShapeDtypeStruct((headings, steps, nodes), jnp.bfloat16),
        in_specs=[pl.BlockSpec((tall, depth), lambda h, t: (t, 0)),
                  pl.BlockSpec((1, depth, nodes), lambda h, t: (h, 0, 0))],
        out_specs=pl.BlockSpec((1, tall, nodes), lambda h, t: (h, t, 0)),
        compiler_params=pltpu.CompilerParams(vmem_limit_bytes=32 * 1024 * 1024),
        name="load_series",
    )(basis, m)


def slot_members(tile_ids, tile_count, capacity):
    row_count = tile_ids.shape[0]
    onehot = (tile_ids[:, None] == jnp.arange(tile_count, dtype=jnp.int32)[None, :]).astype(
        jnp.int32
    )
    slot_rank = jnp.sum((jnp.cumsum(onehot, axis=0) - onehot) * onehot, axis=1)
    slot_index = tile_ids * capacity + slot_rank
    empty = jnp.full((tile_count * capacity,), row_count, jnp.int32)
    return empty.at[slot_index].set(jnp.arange(row_count, dtype=jnp.int32))


def wide_shards(pressure, spectrum_amp, phase_code, panel_tile, patch_weight):
    regrouped = lax.all_to_all(pressure, "freq", split_axis=3, concat_axis=1, tiled=True)
    scaled = scale_spectra(regrouped, spectrum_amp, phase_code)
    freq_count = scaled.shape[1]
    headings = scaled.shape[2]
    panels = scaled.shape[3]
    owners = lax.axis_size("freq")
    windows = lax.axis_size("node")
    window_len = TSTEPS // windows
    first_step = lax.axis_index("node") * window_len
    tile_count = owners * TILE_DEV
    capacity = max(2, 3 * windows * panels // (2 * TILE_DEV * owners))
    tile_ids = panel_tile.reshape(-1)
    weights = patch_weight.reshape(-1, 128)
    members = slot_members(tile_ids, tile_count, capacity)
    sent_weight = jnp.take(weights, members, axis=0, mode="fill", fill_value=0)
    sent_weight = sent_weight.reshape(1, owners, TILE_DEV, capacity, 128)
    spectra = lax.all_gather(scaled, "node", axis=3, tiled=True)
    sent_spectra = jnp.take(spectra, members, axis=3, mode="fill", fill_value=0)
    sent_spectra = sent_spectra.reshape(2 * freq_count * headings, owners, TILE_DEV, capacity)
    wave_basis = basis_table(first_step, window_len)
    got_spectra = lax.all_to_all(sent_spectra, "freq", split_axis=1, concat_axis=1, tiled=True)
    got_weight = lax.all_to_all(sent_weight, "freq", split_axis=1, concat_axis=1, tiled=True)
    shaped = got_spectra.reshape((2 * freq_count, headings) + got_spectra.shape[1:])
    series = jnp.einsum(
        "qhskc,qt->hskct", shaped, wave_basis, preferred_element_type=jnp.float32
    ).astype(jnp.bfloat16)
    partial_value = jnp.einsum(
        "hskct,skcn->htkn", series, got_weight[0], preferred_element_type=jnp.float32
    )
    node_loads = partial_value.reshape(partial_value.shape[0], partial_value.shape[1], -1)
    return node_loads.astype(jnp.bfloat16)


def shards(pressure, spectrum_amp, phase_code, panel_tile, patch_weight):
    owners = lax.axis_size("freq")
    windows = lax.axis_size("node")
    length = panel_tile.shape[1] * panel_tile.shape[2]
    capacity = 3 * length // (2 * TILE_DEV * owners)
    block_bytes = owners * owners * TILE_DEV * SLOT * 128 * (128 // SLOT) * 2
    if capacity > SLOT or block_bytes > 20 * 1024 * 1024:
        return wide_shards(pressure, spectrum_amp, phase_code, panel_tile, patch_weight)
    freqs, headings, panels = pressure.shape[1:]
    first = lax.axis_index("freq") * freqs
    amp = lax.dynamic_slice_in_dim(spectrum_amp, first, freqs, 1)
    code = lax.dynamic_slice_in_dim(phase_code, first, freqs, 1)
    scaled = scale_spectra(pressure, amp, code)
    x = jnp.transpose(scaled, (2, 0, 1, 3)).reshape(headings * 2 * freqs, panels)
    m = node_spectra(x, patch_weight.reshape(length, 128), slot_rows(panel_tile), owners, windows, headings, freqs)
    window_len = TSTEPS // windows
    basis = basis_rows(lax.axis_index("node") * window_len, window_len)
    return load_series(basis, m.reshape(headings, 2 * F, TILE_DEV * 128))


def solution(mesh):
    placed = (
        P(None, "freq", None, "node"),
        P(),
        P(),
        P("freq", None, None, None),
        P("freq", None, None, None),
    )
    return jax.shard_map(
        shards, mesh=mesh, in_specs=placed, out_specs=P(None, "node", "freq"), check_vma=False
    )
```

```python
import functools
import math

import jax
import jax.numpy as jnp
from jax import lax
from jax.experimental import pallas as pl
from jax.experimental.pallas import tpu as pltpu
from jax.sharding import PartitionSpec as P

F = 128
TSTEPS = 4096
BIN_STEP = 15
PHASE_LEVELS = 4096
TILE_DEV = 8
SLOT = 32
MESH = pl.DeviceIdType.MESH


def scale_spectra(pressure, spectrum_amp, phase_code):
    phase_angle = phase_code.astype(jnp.float32) * (2.0 * math.pi / PHASE_LEVELS)
    amplitude = spectrum_amp.T[:, :, None]
    cosine = jnp.cos(phase_angle).T[:, :, None]
    sine_part = jnp.sin(phase_angle).T[:, :, None]
    real_part = pressure[0].astype(jnp.float32)
    imag_part = pressure[1].astype(jnp.float32)
    scaled_re = amplitude * (real_part * cosine - imag_part * sine_part)
    scaled_im = amplitude * (real_part * sine_part + imag_part * cosine)
    return jnp.stack([scaled_re, scaled_im]).astype(jnp.bfloat16)


def basis_table(first_step, step_count):
    freq_bin = 1 + BIN_STEP * jnp.arange(F, dtype=jnp.int32)
    step_ids = first_step + jnp.arange(step_count, dtype=jnp.int32)
    turn_count = freq_bin[:, None] * step_ids[None, :] % TSTEPS
    turn_angle = turn_count.astype(jnp.float32) * (2.0 * math.pi / TSTEPS)
    return jnp.concatenate([jnp.cos(turn_angle), -jnp.sin(turn_angle)], axis=0).astype(jnp.bfloat16)


def basis_rows(first_step, step_count):
    freq_bin = 1 + BIN_STEP * jnp.arange(F, dtype=jnp.int32)
    step_ids = first_step + jnp.arange(step_count, dtype=jnp.int32)
    turn_count = step_ids[:, None] * freq_bin[None, :] % TSTEPS
    turn_angle = turn_count.astype(jnp.float32) * (2.0 * math.pi / TSTEPS)
    return jnp.concatenate([jnp.cos(turn_angle), -jnp.sin(turn_angle)], axis=1).astype(jnp.bfloat16)


def slot_rows(panel_tile):
    tile_ids = panel_tile.reshape(-1)
    count = tile_ids.shape[0]
    order = jnp.arange(count, dtype=jnp.int32)
    same = (tile_ids[:, None] == tile_ids[None, :]) & (order[:, None] < order[None, :])
    rank = jnp.sum(same.astype(jnp.int32), axis=0)
    return (tile_ids * SLOT + rank).reshape(1, count)


def load_kernel(owners, windows, x_ref, w_ref, s_ref, out_ref, xall, sall, cols, xs, ws, block, m,
                z_send, z_recv, w_send, w_recv, o_send, o_recv, s_send, s_recv, m_send, m_recv, own_sem):
    me = lax.axis_index("freq")
    z = lax.axis_index("node")
    rows, panels = x_ref.shape
    part = panels // owners
    groups = xs.shape[0]
    per_group = 128 // SLOT
    group_dev = groups // owners
    chips = owners // 2
    other = me + 1 - 2 * lax.rem(me, 2)

    barrier = pltpu.get_barrier_semaphore()
    for d in range(1, owners):
        pl.semaphore_signal(barrier, inc=1, device_id=(lax.rem(me + d, owners), z), device_id_type=MESH)
    for d in range(1, windows):
        pl.semaphore_signal(barrier, inc=1, device_id=(me, lax.rem(z + d, windows)), device_id_type=MESH)
    pl.semaphore_wait(barrier, owners + windows - 2)

    headings = m.shape[1]
    each = rows // headings
    cuts = [0, headings // 2, headings] if headings > 1 else [0, headings]
    chunks = len(cuts) - 1

    def rows_of(c):
        return slice(cuts[c] * each, cuts[c + 1] * each)

    def z_copy(c, b, source, way, target):
        return pltpu.make_async_remote_copy(
            src_ref=source.at[rows_of(c)], dst_ref=xall.at[b, rows_of(c)], send_sem=z_send.at[way, c, b],
            recv_sem=z_recv.at[c, b], device_id=(me, target), device_id_type=MESH)

    def own_up(c):
        z_copy(c, z, x_ref, 0, z + 1).start()

    def own_down(c):
        z_copy(c, z, x_ref, 1, z - 1).start()

    def s_copy(g, d):
        return pltpu.make_async_remote_copy(
            src_ref=s_ref, dst_ref=sall.at[g], send_sem=s_send.at[d], recv_sem=s_recv.at[d],
            device_id=(lax.rem(me + d, owners), z), device_id_type=MESH)

    def lanes_of(g):
        return pl.ds(pl.multiple_of(g * 128, 128), 128)

    def w_copy(g, d):
        held = ws.at[:, lanes_of(g)]
        return pltpu.make_async_remote_copy(
            src_ref=held, dst_ref=held, send_sem=w_send.at[d], recv_sem=w_recv.at[d],
            device_id=(lax.rem(me + 2 * d, owners), z), device_id_type=MESH)

    def o_copy(g, d):
        held = ws.at[:, lanes_of(g)]
        return pltpu.make_async_remote_copy(
            src_ref=held, dst_ref=held, send_sem=o_send.at[d], recv_sem=o_recv.at[d],
            device_id=(other, z), device_id_type=MESH)

    @pl.when(z + 1 < windows)
    def _():
        own_up(0)

    @pl.when(z > 0)
    def _():
        own_down(0)

    for d in range(1, owners):
        s_copy(me, d).start()
    sall[pl.ds(me, 1)] = s_ref[...][None]

    def weigh(u, carry):
        ids = u * 128 + lax.broadcasted_iota(jnp.int32, (128, s_ref.shape[1]), 0)
        pick = jnp.where(ids == s_ref[...], 1.0, 0.0).astype(jnp.bfloat16)
        ws[u, lanes_of(me)] = jnp.dot(pick, w_ref[...], preferred_element_type=jnp.float32).astype(jnp.bfloat16)
        return carry

    lax.fori_loop(0, groups, weigh, 0)
    for d in range(1, chips):
        w_copy(me, d).start()
    o_copy(me, 0).start()

    for d in range(1, owners):
        s_copy(lax.rem(me + owners - d, owners), d).wait_recv()

    def column(g, carry):
        row = sall[g].astype(jnp.float32)
        for k in range(row.shape[1] // 128):
            piece = jnp.broadcast_to(row[:, k * 128:(k + 1) * 128], (128, 128))
            group = jnp.floor(piece * (1.0 / 128.0)).T
            place_in = piece.T - 128.0 * group
            lane = lax.broadcasted_iota(jnp.int32, (128, 128), 1).astype(jnp.float32)
            cols[g, k * 128:(k + 1) * 128] = jnp.where(place_in == lane, group, -1.0).astype(jnp.bfloat16)
        return carry

    lax.fori_loop(0, owners, column, 0)

    wide = 256 // 128

    def place(c, source, b, fresh):
        held = rows_of(c)

        def one(g, carry):
            x = source[held, pl.ds(pl.multiple_of(g * part, part), part)]
            col = cols[g, pl.ds(pl.multiple_of(b * part, part), part)]
            lanes = lanes_of(g)
            one_hot, empty = jnp.ones_like(col), jnp.zeros_like(col)
            for u in range(0, groups, wide):
                pick = jnp.concatenate(
                    [jnp.where(col == jnp.bfloat16(u + v), one_hot, empty) for v in range(wide)],
                    axis=1)
                got = jnp.dot(x, pick, preferred_element_type=jnp.float32).astype(jnp.bfloat16)
                for v in range(wide):
                    piece = got[:, v * 128:(v + 1) * 128]
                    if fresh:
                        xs[u + v, held, lanes] = piece
                    else:
                        xs[u + v, held, lanes] = xs[u + v, held, lanes] + piece
            return carry

        lax.fori_loop(0, owners, one, 0)

    def arrive(c, s):
        low, high = z - s, z + s

        @pl.when(low >= 0)
        def _():
            z_copy(c, low, xall.at[low], 0, z).wait_recv()

            @pl.when(z + 1 < windows)
            def _():
                z_copy(c, low, xall.at[low], 0, z + 1).start()

        @pl.when(high < windows)
        def _():
            z_copy(c, high, xall.at[high], 1, z).wait_recv()

            @pl.when(z > 0)
            def _():
                z_copy(c, high, xall.at[high], 1, z - 1).start()

        if c + 1 < chunks:
            up_now = z == s
            down_now = windows - 1 - z == s
            if s == 1:
                up_now = up_now | (z == 0)
                down_now = down_now | (z == windows - 1)

            @pl.when(up_now & (z + 1 < windows))
            def _():
                own_up(c + 1)

            @pl.when(down_now & (z > 0))
            def _():
                own_down(c + 1)

    def settle(c, s):
        low, high = z - s, z + s

        @pl.when(low >= 0)
        def _():
            place(c, xall.at[low], low, False)

        @pl.when(high < windows)
        def _():
            place(c, xall.at[high], high, False)

    def spread():
        part_of = lax.rem(lax.broadcasted_iota(jnp.int32, (128, 128), 0) // SLOT, per_group)

        def one(u, carry):
            for g in range(owners):
                w = ws[u, g * 128:(g + 1) * 128]
                for tt in range(per_group):
                    block[u, g * 128:(g + 1) * 128, tt * 128:(tt + 1) * 128] = jnp.where(
                        part_of == tt, w, jnp.zeros_like(w))
            return carry

        lax.fori_loop(0, groups, one, 0)

    def gather_loads(c, target):
        def one(e, carry):
            u = target * group_dev + e
            width = per_group * 128
            got = jnp.dot(xs[u, rows_of(c)], block[u], preferred_element_type=jnp.float32).astype(jnp.bfloat16)
            m[target, cuts[c]:cuts[c + 1], :, :, pl.ds(pl.multiple_of(e * width, width), width)] = got.reshape(
                (cuts[c + 1] - cuts[c],) + m.shape[2:4] + (width,))
            return carry

        lax.fori_loop(0, group_dev, one, 0)

    def m_copy(c, d, source, dest, device):
        return pltpu.make_async_remote_copy(
            src_ref=m.at[source, cuts[c]:cuts[c + 1]], dst_ref=out_ref.at[cuts[c]:cuts[c + 1], :, dest],
            send_sem=m_send.at[c, d], recv_sem=m_recv.at[c, d], device_id=(device, z), device_id_type=MESH)

    def sent(c, d):
        target = lax.rem(me + d, owners)
        return m_copy(c, d, target, me, target)

    def hand_out(c, first, last):
        for d in range(max(first, 1), last):
            gather_loads(c, lax.rem(me + d, owners))
            sent(c, d).start()
        if last == owners:
            gather_loads(c, me)

    for c in range(chunks):
        place(c, x_ref, z, True)
        for s in range(1, windows):
            arrive(c, s)
            if c == 1 and s == 1:
                for d in range(chips):
                    o_copy(lax.rem(other + owners - 2 * d, owners), d).wait_recv()
                spread()
                hand_out(0, 1, owners // 2)
                if windows > 2:
                    continue
            if c == 1 and s == min(2, windows - 1):
                hand_out(0, owners // 2, owners)
                if s == 2:
                    settle(c, 1)
            settle(c, s)
        if c == 0:
            for d in range(1, chips):
                src = lax.rem(me + owners - 2 * d, owners)
                w_copy(src, d).wait_recv()
                o_copy(src, d).start()
        if chunks == 1:
            for d in range(chips):
                o_copy(lax.rem(other + owners - 2 * d, owners), d).wait_recv()
            spread()
        if c or chunks == 1:
            hand_out(c, 1, owners)
    own = pltpu.make_async_copy(m.at[me], out_ref.at[:, :, me], own_sem)
    own.start()
    own.wait()

    for c in range(chunks):
        for d in range(1, owners):
            src = lax.rem(me + owners - d, owners)
            m_copy(c, d, src, src, src).wait_recv()
            sent(c, d).wait_send()
    for d in range(1, owners):
        s_copy(me, d).wait_send()
    for d in range(1, chips):
        w_copy(me, d).wait_send()
    for d in range(chips):
        o_copy(me, d).wait_send()
    for s in range(windows):
        low, high = z - s, z + s

        @pl.when((low >= 0) & (z + 1 < windows))
        def _():
            for c in range(chunks):
                z_copy(c, low, x_ref, 0, z + 1).wait_send()

        @pl.when((high < windows) & (z > 0))
        def _():
            for c in range(chunks):
                z_copy(c, high, x_ref, 1, z - 1).wait_send()


def node_spectra(x, w, s, owners, windows, headings, freqs):
    rows, panels = x.shape
    groups = owners * TILE_DEV * SLOT // 128
    length = w.shape[0]
    dma = pltpu.SemaphoreType.DMA
    vmem = pl.BlockSpec(memory_space=pltpu.VMEM)
    nodes = TILE_DEV * 128
    return pl.pallas_call(
        functools.partial(load_kernel, owners, windows),
        out_shape=jax.ShapeDtypeStruct((headings, 2, owners, freqs, nodes), jnp.bfloat16),
        in_specs=[vmem] * 3,
        out_specs=vmem,
        scratch_shapes=[
            pltpu.VMEM((windows, rows, panels), jnp.bfloat16),
            pltpu.VMEM((owners, 1, length), jnp.int32),
            pltpu.VMEM((owners, length, 128), jnp.bfloat16),
            pltpu.VMEM((groups, rows, owners * 128), jnp.bfloat16),
            pltpu.VMEM((groups, owners * 128, 128), jnp.bfloat16),
            pltpu.VMEM((groups, owners * 128, 128 // SLOT * 128), jnp.bfloat16),
            pltpu.VMEM((owners, headings, 2, freqs, nodes), jnp.bfloat16),
            dma((2, headings, windows)), dma((headings, windows)),
            dma((owners,)), dma((owners,)), dma((owners,)), dma((owners,)), dma((owners,)), dma((owners,)),
            dma((headings, owners)), dma((headings, owners)),
            dma(()),
        ],
        compiler_params=pltpu.CompilerParams(
            collective_id=0, has_side_effects=True, vmem_limit_bytes=56 * 1024 * 1024),
        name="node_spectra",
    )(x, w, s)


def series_kernel(basis_ref, m_ref, out_ref):
    out_ref[0] = jnp.dot(basis_ref[...], m_ref[0], preferred_element_type=jnp.float32).astype(out_ref.dtype)


def load_series(basis, m):
    steps, depth = basis.shape
    headings, _, nodes = m.shape
    tall = 512
    return pl.pallas_call(
        series_kernel,
        grid=(headings, steps // tall),
        out_shape=jax.ShapeDtypeStruct((headings, steps, nodes), jnp.bfloat16),
        in_specs=[pl.BlockSpec((tall, depth), lambda h, t: (t, 0)),
                  pl.BlockSpec((1, depth, nodes), lambda h, t: (h, 0, 0))],
        out_specs=pl.BlockSpec((1, tall, nodes), lambda h, t: (h, t, 0)),
        compiler_params=pltpu.CompilerParams(vmem_limit_bytes=32 * 1024 * 1024),
        name="load_series",
    )(basis, m)


def slot_members(tile_ids, tile_count, capacity):
    row_count = tile_ids.shape[0]
    onehot = (tile_ids[:, None] == jnp.arange(tile_count, dtype=jnp.int32)[None, :]).astype(
        jnp.int32
    )
    slot_rank = jnp.sum((jnp.cumsum(onehot, axis=0) - onehot) * onehot, axis=1)
    slot_index = tile_ids * capacity + slot_rank
    empty = jnp.full((tile_count * capacity,), row_count, jnp.int32)
    return empty.at[slot_index].set(jnp.arange(row_count, dtype=jnp.int32))


def wide_shards(pressure, spectrum_amp, phase_code, panel_tile, patch_weight):
    regrouped = lax.all_to_all(pressure, "freq", split_axis=3, concat_axis=1, tiled=True)
    scaled = scale_spectra(regrouped, spectrum_amp, phase_code)
    freq_count = scaled.shape[1]
    headings = scaled.shape[2]
    panels = scaled.shape[3]
    owners = lax.axis_size("freq")
    windows = lax.axis_size("node")
    window_len = TSTEPS // windows
    first_step = lax.axis_index("node") * window_len
    tile_count = owners * TILE_DEV
    capacity = max(2, 3 * windows * panels // (2 * TILE_DEV * owners))
    tile_ids = panel_tile.reshape(-1)
    weights = patch_weight.reshape(-1, 128)
    members = slot_members(tile_ids, tile_count, capacity)
    sent_weight = jnp.take(weights, members, axis=0, mode="fill", fill_value=0)
    sent_weight = sent_weight.reshape(1, owners, TILE_DEV, capacity, 128)
    spectra = lax.all_gather(scaled, "node", axis=3, tiled=True)
    sent_spectra = jnp.take(spectra, members, axis=3, mode="fill", fill_value=0)
    sent_spectra = sent_spectra.reshape(2 * freq_count * headings, owners, TILE_DEV, capacity)
    wave_basis = basis_table(first_step, window_len)
    got_spectra = lax.all_to_all(sent_spectra, "freq", split_axis=1, concat_axis=1, tiled=True)
    got_weight = lax.all_to_all(sent_weight, "freq", split_axis=1, concat_axis=1, tiled=True)
    shaped = got_spectra.reshape((2 * freq_count, headings) + got_spectra.shape[1:])
    series = jnp.einsum(
        "qhskc,qt->hskct", shaped, wave_basis, preferred_element_type=jnp.float32
    ).astype(jnp.bfloat16)
    partial_value = jnp.einsum(
        "hskct,skcn->htkn", series, got_weight[0], preferred_element_type=jnp.float32
    )
    node_loads = partial_value.reshape(partial_value.shape[0], partial_value.shape[1], -1)
    return node_loads.astype(jnp.bfloat16)


def shards(pressure, spectrum_amp, phase_code, panel_tile, patch_weight):
    owners = lax.axis_size("freq")
    windows = lax.axis_size("node")
    length = panel_tile.shape[1] * panel_tile.shape[2]
    capacity = 3 * length // (2 * TILE_DEV * owners)
    block_bytes = owners * owners * TILE_DEV * SLOT * 128 * (128 // SLOT) * 2
    if capacity > SLOT or block_bytes > 20 * 1024 * 1024 or owners * TILE_DEV * SLOT > 128 * 256:
        return wide_shards(pressure, spectrum_amp, phase_code, panel_tile, patch_weight)
    freqs, headings, panels = pressure.shape[1:]
    first = lax.axis_index("freq") * freqs
    amp = lax.dynamic_slice_in_dim(spectrum_amp, first, freqs, 1)
    code = lax.dynamic_slice_in_dim(phase_code, first, freqs, 1)
    scaled = scale_spectra(pressure, amp, code)
    x = jnp.transpose(scaled, (2, 0, 1, 3)).reshape(headings * 2 * freqs, panels)
    m = node_spectra(x, patch_weight.reshape(length, 128), slot_rows(panel_tile), owners, windows, headings, freqs)
    window_len = TSTEPS // windows
    basis = basis_rows(lax.axis_index("node") * window_len, window_len)
    return load_series(basis, m.reshape(headings, 2 * F, TILE_DEV * 128))


def solution(mesh):
    placed = (
        P(None, "freq", None, "node"),
        P(),
        P(),
        P("freq", None, None, None),
        P("freq", None, None, None),
    )
    return jax.shard_map(
        shards, mesh=mesh, in_specs=placed, out_specs=P(None, "node", "freq"), check_vma=False
    )
```
